32 devices in a mesh: blk: 16 (over z, y, core), cls: 2 (over x).
Axes of the slice: x: 2, y: 2, z: 4, core: 2. Of those that a mesh axis runs over, the one named last changes fastest.
Arguments:
- features: bfloat16 [1024, 2048], P('blk'), may hold values from -6 to 6
- labels: int32 [1024], P('blk'), may hold values from 0 to 655359
- offset: int32 [1], replicated, may hold values from 0 to 524288
- other_lse: float32 [1024], replicated, may hold values from 15 to 20
- weight: bfloat16 [131072, 2048], P(('blk', 'cls'))
- accum: float32 [131072, 2048], P(('blk', 'cls')), may hold values from 0.1 to 1
Outputs:
- new_weight: bfloat16 [131072, 2048], P(('blk', 'cls'))
- new_accum: float32 [131072, 2048], P(('blk', 'cls'))
- lse: float32 [1024], P('blk')
The draws below stay inside these ranges and needn't reach their ends.
All inputs are finite; a program needn't handle non-finite values.
Results may differ from the reference program's by a relative error of at most 0.004.
Values may be sent and summed in bfloat16 or wider, within the bound.
No kernel may reach another device: no remote copies, remote signals or barrier semaphores. Data moves between devices by JAX's collectives and lax.ppermute only.
A program may use at most 192 MiB of HBM per device.

```python
import math
import jax
import jax.numpy as jnp
from jax import lax

F = 2048
CLASSES = 131072
ALL_CLASSES = 655360
BATCH = 1024


def draw_features(key, part):
    key_base = jax.random.fold_in(key, 0)
    base = jax.random.truncated_normal(key_base, -4.0, 4.0, (BATCH, F), jnp.float32)
    return base.astype(jnp.bfloat16)


def draw_weight(key, part):
    base = jax.random.truncated_normal(key, -4.0, 4.0, (CLASSES, F), jnp.float32)
    place = (jnp.arange(CLASSES, dtype=jnp.float32) / CLASSES)[:, None]
    sigma = 1.3 * jnp.exp(place * jnp.log(3.0))
    return (base * sigma * F ** (-0.5)).astype(jnp.bfloat16)


def set_ends(values, key, least, high):
    spot = [jax.random.randint(jax.random.fold_in(key, axis), (), 0, length) for axis, length in enumerate(values.shape)]
    longest = values.shape.index(max(values.shape))
    neighbour = spot[:longest] + [(spot[longest] + 1) % values.shape[longest]] + spot[longest + 1:]
    return values.at[tuple(spot)].set(least).at[tuple(neighbour)].set(high)


def block_levels(key, dims, cuts, low, largest):
    def one(axis_at, parts):
        heights = jax.random.uniform(jax.random.fold_in(jax.random.fold_in(key, 6), axis_at), (parts,), jnp.float32, low / len(cuts), largest / len(cuts))
        return jnp.repeat(jnp.exp(heights), dims[axis_at] // parts).reshape((-1,) + (1,) * (len(dims) - axis_at - 1))

    gain = one(*cuts[0])
    for cut in cuts[1:]:
        gain = gain * one(*cut)
    return gain


def setup_inputs(seed: int = 0) -> dict:
    key_of = jax.random.split(jax.random.key(seed), 7)
    return {
        "features": draw_features(jax.random.fold_in(key_of[6], 71), 0),
        "labels": set_ends(jax.random.randint(key_of[1], (BATCH,), 0, ALL_CLASSES), jax.random.fold_in(key_of[1], 1), 0, ALL_CLASSES - 1).astype(jnp.int32),
        "offset": jax.random.randint(key_of[2], (1,), 0, ALL_CLASSES - CLASSES + 1).astype(jnp.int32),
        "other_lse": jnp.clip(jax.random.uniform(key_of[3], (BATCH,), jnp.float32, 15.0, 20.0), 15.0, 20.0),
        "weight": draw_weight(jax.random.fold_in(key_of[6], 71), 0),
        "accum": jnp.clip(jnp.exp(math.log(1.0) - 2.3025851 * jax.random.uniform(key_of[5], (CLASSES, F), jnp.float32) ** block_levels(key_of[5], (CLASSES, F), ((0, 32),), -0.2, 0.2)), 0.1, 1.0),
    }


def reference(features, labels, offset, other_lse, weight, accum):
    span = min(CLASSES, 8192)
    count = CLASSES // span
    w_blocks = weight.reshape(count, span, F)
    a_blocks = accum.reshape(count, span, F)
    starts = jnp.arange(count, dtype=jnp.int32) * span

    def logit_block(w_block):
        return lax.dot_general(features, w_block, (((1,), (1,)), ((), ())), preferred_element_type=jnp.float32)

    def stats(w_block):
        logits = logit_block(w_block)
        block_top = lax.optimization_barrier(jnp.max(logits, axis=1))
        block_total = lax.optimization_barrier(jnp.sum(jnp.exp(logits - block_top[:, None]), axis=1))
        return (block_top, block_total)
    tops, totals = lax.map(stats, w_blocks)
    top = lax.optimization_barrier(jnp.max(tops, axis=0))
    total = lax.optimization_barrier(jnp.sum(totals * jnp.exp(tops - top[None, :]), axis=0))
    slab_lse = top + jnp.log(total)
    high = jnp.maximum(slab_lse, other_lse)
    lse = high + jnp.log(jnp.exp(slab_lse - high) + jnp.exp(other_lse - high))

    def update(items):
        w_block, a_block, start = items
        logits = logit_block(w_block)
        local = (labels - offset[0] - start).astype(jnp.int32)
        onehot = (local[:, None] == jnp.arange(span, dtype=jnp.int32)[None, :]).astype(jnp.float32)
        delta = (jnp.exp(logits - lse[:, None]) - onehot).astype(jnp.bfloat16)
        grad = lax.dot_general(delta, features, (((0,), (0,)), ((), ())), preferred_element_type=jnp.float32)
        acc_next = a_block + grad * grad
        w_next = (w_block.astype(jnp.float32) - 0.05 * grad / (jnp.sqrt(acc_next) + 1e-10)).astype(jnp.bfloat16)
        return (w_next, acc_next)
    w_new, a_new = lax.map(update, (w_blocks, a_blocks, starts))
    return (w_new.reshape(CLASSES, F), a_new.reshape(CLASSES, F), lse)
```

```python
import functools

import jax
import jax.numpy as jnp
from jax import lax
from jax.experimental import pallas as pl
from jax.experimental.pallas import tpu as pltpu
from jax.sharding import PartitionSpec as P

f32, bf16, i32 = jnp.float32, jnp.bfloat16, jnp.int32
VM = pl.BlockSpec(memory_space=pltpu.VMEM)
ANY = pl.BlockSpec(memory_space=pl.ANY)
SM = pl.BlockSpec(memory_space=pltpu.SMEM)
MIB = 2**20
LANES = 128
HELD_BYTES = 16 * MIB
LAG = 2
NO_LABEL = -4.0e6
SCOPED = 4 * MIB


def in_vmem(x):
    return pltpu.with_memory_space_constraint(x, pltpu.VMEM)


def in_hbm(x):
    return pltpu.with_memory_space_constraint(x, pltpu.HBM)


def ring_chips(chips):
    half = chips // 2
    return [2 * p if p < half else 2 * (chips - 1 - p) + 1 for p in range(chips)]


def ring_pairs(chips):
    ring = ring_chips(chips)
    pairs = []
    for p in range(chips):
        pairs.append((2 * ring[p], 2 * ring[(p + 1) % chips]))
        pairs.append((2 * ring[p] + 1, 2 * ring[p - 1] + 1))
    return pairs


def chip_at(place, chips):
    place = lax.rem(place + 2 * chips, chips)
    return jnp.where(place < chips // 2, 2 * place, 2 * (chips - 1 - place) + 1)


def whereabouts(chips):
    blk = lax.axis_index("blk")
    chip, core = blk // 2, lax.rem(blk, 2)
    z = chip // 2
    place = jnp.where(lax.rem(chip, 2) == 0, z, chips - 1 - z)
    return chip, core, place


def pair_slots(chips):
    _, core, place = whereabouts(chips)
    sign = 1 - 2 * core
    slots = [(chip_at(place, chips), core)]
    for step in range(1, chips // 2):
        slots.append((chip_at(place - step * sign, chips), core))
        slots.append((chip_at(place + step * sign, chips), 1 - core))
    slots.append((chip_at(place + chips // 2, chips), core))
    return slots


def swapped(row, swap):
    half = row.shape[1] // 2
    other = jnp.concatenate([row[:, half:], row[:, :half]], axis=1)
    return jnp.where(swap == 1, other, row)


def merge_parts(messages):
    n = messages[0].shape[0] // 3
    tops = [m[:n] for m in messages]
    top = functools.reduce(jnp.maximum, tops)
    total = sum(m[n : 2 * n] * jnp.exp(t - top) for m, t in zip(messages, tops))
    return top, total, functools.reduce(jnp.maximum, [m[2 * n :] for m in messages])


def hold_kernel(chips, pieces, w_hbm, pair_hbm, labels_hbm, offset_ref, *refs):
    w_ref, _, x_ref, _, msg_ref, labels_ref, sem, pair_sem, label_sem = refs
    rows = w_ref.shape[0] // pieces
    copies = [
        pltpu.make_async_copy(
            w_hbm.at[pl.ds(i * rows, rows)], w_ref.at[pl.ds(i * rows, rows)], sem.at[i]
        )
        for i in range(pieces)
    ]
    label_copy = pltpu.make_async_copy(labels_hbm, labels_ref, label_sem)
    label_copy.start()
    pair_copy = pltpu.make_async_copy(
        pair_hbm, x_ref.at[pl.ds(0, pair_hbm.shape[0])], pair_sem
    )
    pair_copy.start()
    for copy in copies:
        copy.start()
    label_copy.wait()
    msg_ref[: 2 * chips] = jnp.zeros((2 * chips, LANES), f32)
    msg_ref[2 * chips :] = jnp.full((chips, LANES), NO_LABEL, f32)
    mine = (labels_ref[...] - offset_ref[0]).astype(f32)
    none = jnp.full_like(mine, NO_LABEL)
    chip, core, _ = whereabouts(chips)
    msg_ref[pl.ds(2 * chips + chip, 1), :] = jnp.concatenate(
        [jnp.where(core == 0, mine, none), jnp.where(core == 0, none, mine)], axis=1
    )
    for copy in copies:
        copy.wait()
    pair_copy.wait()


def hold(weight, pair, labels, offset, chips, batch, held_rows):
    pieces = 4
    rows, feats = weight.shape
    labels = labels.reshape(1, -1)
    return pl.pallas_call(
        functools.partial(hold_kernel, chips, pieces),
        name="hold_weight",
        out_shape=[
            pltpu.VMEM((rows, feats), bf16),
            pltpu.VMEM((rows, batch), f32),
            pltpu.VMEM((batch, feats), bf16),
            pltpu.VMEM((held_rows, feats), f32),
            pltpu.VMEM((3 * chips, LANES), f32),
        ],
        in_specs=[ANY, ANY, ANY, SM],
        out_specs=[VM] * 5,
        scratch_shapes=[
            pltpu.VMEM(labels.shape, i32),
            pltpu.SemaphoreType.DMA((pieces,)),
            pltpu.SemaphoreType.DMA,
            pltpu.SemaphoreType.DMA,
        ],
        compiler_params=pltpu.CompilerParams(vmem_limit_bytes=SCOPED),
        cost_estimate=pl.CostEstimate(
            flops=0, bytes_accessed=weight.size * 2, transcendentals=0
        ),
    )(in_hbm(weight), in_hbm(pair), in_hbm(labels), offset)


def fold(op, values):
    return op(values.reshape(values.shape[0] // 8, 8, values.shape[1]), axis=0)


def more_stats(logits, top, total):
    new_top = jnp.maximum(top, fold(jnp.max, logits))
    terms = jnp.exp(logits.reshape(logits.shape[0] // 8, 8, logits.shape[1]) - new_top[None])
    return new_top, total * jnp.exp(top - new_top) + jnp.sum(terms, axis=0)


def score_kernel(cfg, *refs):
    chips, k, held, bm, n_blocks = cfg
    blocks, accum_hbm, refs = refs[:n_blocks], refs[n_blocks], refs[n_blocks + 1 :]
    msg_in, refs = refs[0], refs[5:]
    msg_ref, w_ref, logits_ref, x_ref, acc_ref, acc_sem, x_sem = refs
    rows, width = w_ref.shape[0], 2 * LANES
    columns = pl.ds(k * width, width)
    accum_copy = None
    if held[1] > held[0]:
        part = pl.ds(held[0], held[1] - held[0])
        accum_copy = pltpu.make_async_copy(accum_hbm.at[part], acc_ref.at[part], acc_sem)
        accum_copy.start()
    if k == 0:
        copy = pltpu.make_async_copy(blocks[0], x_ref.at[pl.ds(LANES, LANES)], x_sem)
        copy.start()
        copy.wait()
    else:
        at = k * width
        for block in blocks:
            x_ref[pl.ds(at, block.shape[0]), :] = block[...]
            at += block.shape[0]
    x = x_ref.at[columns]
    top = jnp.full((8, width), -3.0e38, f32)
    total = jnp.zeros((8, width), f32)
    for i in range(rows // bm):
        logits_ref[pl.ds(i * bm, bm), columns] = lax.dot_general(
            w_ref[pl.ds(i * bm, bm), :],
            x[...],
            (((1,), (1,)), ((), ())),
            preferred_element_type=f32,
        )
        if i > 0:
            top, total = more_stats(logits_ref[pl.ds((i - 1) * bm, bm), columns], top, total)
    top, total = more_stats(logits_ref[pl.ds(rows - bm, bm), columns], top, total)
    one_top = jnp.max(top, axis=0, keepdims=True)
    one_total = jnp.sum(total * jnp.exp(top - one_top), axis=0, keepdims=True)
    msg_ref[...] = msg_in[...]
    slots = pair_slots(chips)[2 * k : 2 * k + 2]
    for j, (owner, swap) in enumerate(slots):
        lanes = slice(j * LANES, (j + 1) * LANES)
        msg_ref[pl.ds(owner, 1), :] = swapped(one_top[:, lanes], swap)
        msg_ref[pl.ds(chips + owner, 1), :] = swapped(one_total[:, lanes], swap)
    if accum_copy is not None:
        accum_copy.wait()


def score(k, chips, blocks, accum, held, state):
    rows, feats = state[1].shape
    bm = min(512, rows)
    width = 2 * LANES
    base = len(blocks) + 2
    place = in_hbm if k == 0 else in_vmem
    inputs = [place(b) for b in blocks] + [in_hbm(accum)] + [in_vmem(s) for s in state]
    specs = [ANY if k == 0 else VM] * len(blocks) + [ANY]
    aliases = {base + i: 1 + i for i in range(4)}
    specs += [VM] * (len(inputs) - len(specs))
    cfg = (chips, k, held, bm, len(blocks))
    return pl.pallas_call(
        functools.partial(score_kernel, cfg),
        name=f"score_{k}",
        out_shape=[pltpu.VMEM(a.shape, a.dtype) for a in state],
        in_specs=specs,
        out_specs=[VM] * 5,
        input_output_aliases=aliases,
        scratch_shapes=[pltpu.SemaphoreType.DMA, pltpu.SemaphoreType.DMA],
        compiler_params=pltpu.CompilerParams(vmem_limit_bytes=SCOPED),
        cost_estimate=pl.CostEstimate(
            flops=2 * rows * feats * width,
            bytes_accessed=(rows + width) * feats * 2,
            transcendentals=rows * width,
        ),
    )(*inputs)


def small_call(kernel, name, shape, inputs, pinned):
    n = len(inputs)

    def with_pinned(*refs):
        kernel(*refs[:n], refs[n + len(pinned)])

    out, *pinned = pl.pallas_call(
        with_pinned,
        name=name,
        out_shape=[pltpu.VMEM(shape, inputs[0].dtype)]
        + [pltpu.VMEM(p.shape, p.dtype) for p in pinned],
        in_specs=[VM] * (n + len(pinned)),
        out_specs=[VM] * (1 + len(pinned)),
        input_output_aliases={n + i: 1 + i for i in range(len(pinned))},
        compiler_params=pltpu.CompilerParams(vmem_limit_bytes=SCOPED),
    )(*[in_vmem(a) for a in [*inputs, *pinned]])
    return out, pinned


def head_kernel(x_ref, out_ref):
    out_ref[...] = x_ref[: out_ref.shape[0], :]


def merge_kernel(*refs):
    top, total, labels = merge_parts([r[...] for r in refs[:-1]])
    n = top.shape[0]
    refs[-1][:n] = top
    refs[-1][n : 2 * n] = total
    refs[-1][2 * n :] = labels


def update_kernel(cfg, *refs):
    chips, n_msgs, bm, held_blocks, bn = cfg
    msgs, refs = refs[:n_msgs], refs[n_msgs:]
    other_ref, accum_hbm, logits_ref, x_ref = refs[:4]
    w_ref, acc_ref, out_w, out_acc, out_lse = refs[6:11]
    canon_s, lse_s, label_s, delta_s, read_sem, acc_sem, w_sem = refs[11:]
    rows, batch = logits_ref.shape
    feats = x_ref.shape[1]
    blocks = rows // bm

    chip, core, _ = whereabouts(chips)
    rank = lax.axis_index("blk") * lax.axis_size("cls") + lax.axis_index("cls")
    first_class = rank * rows
    top, total, labels = merge_parts([m[...] for m in msgs])
    slab_lse = top + jnp.log(total)
    other = other_ref[...]
    high = jnp.maximum(slab_lse, other)
    lse = high + jnp.log(jnp.exp(slab_lse - high) + jnp.exp(other - high))
    canon_s[:chips] = lse
    canon_s[chips:] = labels
    own = canon_s[pl.ds(chip, 1), :]
    out_lse[...] = jnp.where(core == 0, own[:, : LANES // 2], own[:, LANES // 2 :])
    for j, (owner, swap) in enumerate(pair_slots(chips)):
        lanes = pl.ds(j * LANES, LANES)
        lse_s[:, lanes] = swapped(canon_s[pl.ds(owner, 1), :], swap)
        label_s[:, lanes] = (
            swapped(canon_s[pl.ds(chips + owner, 1), :], swap).astype(i32) - first_class
        )

    def make_delta(i, to):
        r0 = pl.multiple_of(i * bm, bm)
        chance = jnp.exp(logits_ref[pl.ds(r0, bm), :] - lse_s[...])
        row = lax.broadcasted_iota(i32, (bm, batch), 0)
        hit = row == (label_s[...] - r0)
        delta_s[to] = jnp.where(hit, chance - 1.0, chance).astype(bf16)

    def rows_of(i):
        return pl.ds(pl.multiple_of(i * bm, bm), bm)

    def read(i):
        slot = lax.rem(i, held_blocks)
        return pltpu.make_async_copy(
            accum_hbm.at[rows_of(i)], acc_ref.at[rows_of(slot)], read_sem.at[slot]
        )

    def writes(i):
        slot = lax.rem(i, held_blocks)
        return (
            pltpu.make_async_copy(
                acc_ref.at[rows_of(slot)], out_acc.at[rows_of(i)], acc_sem.at[slot]
            ),
            pltpu.make_async_copy(
                w_ref.at[rows_of(i)], out_w.at[rows_of(i)], w_sem.at[lax.rem(i, LAG + 1)]
            ),
        )

    make_delta(0, 0)

    def step(i, carry):
        now = lax.rem(i, 2)
        slot = lax.rem(i, held_blocks)

        @pl.when(i >= held_blocks)
        def _():
            read(i).wait()

        make_delta(jnp.minimum(i + 1, blocks - 1), 1 - now)
        for n in range(feats // bn):
            cols = pl.ds(n * bn, bn)
            grad = jnp.dot(delta_s[now], x_ref[:, cols], preferred_element_type=f32)
            new_acc = acc_ref[rows_of(slot), cols] + grad * grad
            acc_ref[rows_of(slot), cols] = new_acc
            old = w_ref[rows_of(i), cols].astype(f32)
            w_ref[rows_of(i), cols] = (
                old - 0.05 * grad / (jnp.sqrt(new_acc) + 1e-10)
            ).astype(bf16)

        @pl.when(i >= LAG)
        def _():
            for copy in writes(i - LAG):
                copy.wait()

            @pl.when(i - LAG + held_blocks < blocks)
            def _():
                read(i - LAG + held_blocks).start()

        for copy in writes(i):
            copy.start()
        return carry

    lax.fori_loop(0, blocks, step, 0)
    for i in range(max(0, blocks - LAG), blocks):
        for copy in writes(i):
            copy.wait()


def update(chips, msgs, other, accum, logits, x, weight_v, acc_v, bm):
    rows, batch = logits.shape
    feats = x.shape[1]
    held_blocks = acc_v.shape[0] // bm
    bn = min(512, feats)
    inputs = [in_vmem(m) for m in msgs] + [other, in_hbm(accum)] + [
        in_vmem(a) for a in (logits, x, weight_v, acc_v)
    ]
    n = len(msgs)
    cfg = (chips, n, bm, held_blocks, bn)
    outs = pl.pallas_call(
        functools.partial(update_kernel, cfg),
        name="update",
        out_shape=[
            pltpu.VMEM(weight_v.shape, bf16),
            pltpu.VMEM(acc_v.shape, f32),
            pltpu.HBM((rows, feats), bf16),
            pltpu.HBM((rows, feats), f32),
            jax.ShapeDtypeStruct((1, LANES // 2), f32),
        ],
        in_specs=[VM] * n + [VM, ANY, VM, VM, VM, VM],
        out_specs=[VM, VM, ANY, ANY, VM],
        input_output_aliases={n + 4: 0, n + 5: 1},
        scratch_shapes=[
            pltpu.VMEM((2 * chips, LANES), f32),
            pltpu.VMEM((1, batch), f32),
            pltpu.VMEM((1, batch), i32),
            pltpu.VMEM((2, bm, batch), bf16),
            pltpu.SemaphoreType.DMA((held_blocks,)),
            pltpu.SemaphoreType.DMA((held_blocks,)),
            pltpu.SemaphoreType.DMA((LAG + 1,)),
        ],
        compiler_params=pltpu.CompilerParams(vmem_limit_bytes=SCOPED),
        cost_estimate=pl.CostEstimate(
            flops=2 * rows * feats * batch,
            bytes_accessed=rows * feats * 10,
            transcendentals=rows * batch,
        ),
    )(*inputs)
    return outs[2:]


def exchange_stats(message, pinned, blk_size, cls_size):
    bits_cls = cls_size.bit_length() - 1
    bits = bits_cls + blk_size.bit_length() - 1
    core, y = bits_cls, bits_cls + 1
    rest = [b for b in range(bits) if b not in (core, y, 0)]
    groups = [(core,), (0, y)] + [tuple(rest[i : i + 2]) for i in range(0, len(rest), 2)]
    messages = [message]
    for group in groups:
        if len(messages) > 1:
            message, pinned = small_call(
                merge_kernel, "merge_stats", message.shape, messages, pinned
            )
        messages = [message]
        for pick in range(1, 2 ** len(group)):
            flip = sum(1 << b for at, b in enumerate(group) if pick >> at & 1)
            pairs = [(d, d ^ flip) for d in range(blk_size * cls_size)]
            messages.append(lax.ppermute(message, ("blk", "cls"), pairs))
    return messages, pinned


def body(features, labels, offset, other_lse, weight, accum):
    blk_size, cls_size = lax.axis_size("blk"), lax.axis_size("cls")
    chips = blk_size // 2
    steps = chips // 2
    block, feats = features.shape
    rows = weight.shape[0]
    batch = block * blk_size
    bm = min(256 * 1024 // batch, rows)
    held_rows = min(rows, HELD_BYTES // (feats * 4))

    def swap_cores(x):
        return lax.ppermute(x, "blk", [(d, d ^ 1) for d in range(blk_size)])

    def round_ring(x):
        return lax.ppermute(x, "blk", ring_pairs(chips))

    sibling = swap_cores(features)
    pair = jnp.concatenate([features, sibling], axis=0)
    came = round_ring(pair)
    *pinned, message = hold(weight, pair, labels, offset, chips, batch, held_rows)
    state = [message, *pinned]
    came, state[0] = lax.optimization_barrier((came, state[0]))
    blocks = [came]
    for k in range(steps):
        if k < steps - 1:
            crossed = swap_cores(came)
            if k == steps - 2:
                came, state[1:] = small_call(head_kernel, "head", (block, feats), [came], state[1:])
            came = round_ring(came)
        cut = [min(held_rows, held_rows * i // 2) for i in (k, k + 1)] if k < 2 else [0, 0]
        state = list(score(k, chips, blocks, accum, tuple(cut), state))
        if k < steps - 1:
            came, state[0] = lax.optimization_barrier((came, state[0]))
            blocks = [crossed, came] + ([swap_cores(came)] if k == steps - 2 else [])
    messages, pinned = exchange_stats(state[0], state[1:], blk_size, cls_size)
    weight_v, logits, x, acc_v = pinned
    new_weight, new_accum, lse = update(
        chips, messages, other_lse.reshape(chips, LANES), accum, logits, x, weight_v, acc_v, bm
    )
    return (new_weight, new_accum, lse.reshape(block))


def solution(mesh):
    in_specs = (
        P("blk", None),
        P("blk"),
        P(),
        P(),
        P(("blk", "cls"), None),
        P(("blk", "cls"), None),
    )
    out_specs = (P(("blk", "cls"), None), P(("blk", "cls"), None), P("blk"))
    return jax.shard_map(body, mesh=mesh, in_specs=in_specs, out_specs=out_specs, check_vma=False)
```

```python
import functools

import jax
import jax.numpy as jnp
from jax import lax
from jax.experimental import pallas as pl
from jax.experimental.pallas import tpu as pltpu
from jax.sharding import PartitionSpec as P

f32, bf16, i32 = jnp.float32, jnp.bfloat16, jnp.int32
VM = pl.BlockSpec(memory_space=pltpu.VMEM)
ANY = pl.BlockSpec(memory_space=pl.ANY)
SM = pl.BlockSpec(memory_space=pltpu.SMEM)
MIB = 2**20
LANES = 128
HELD_BYTES = 20 * MIB
SUB = 32
LAG = 2
NO_LABEL = -4.0e6
SCOPED = 4 * MIB


def in_vmem(x):
    return pltpu.with_memory_space_constraint(x, pltpu.VMEM)


def in_hbm(x):
    return pltpu.with_memory_space_constraint(x, pltpu.HBM)


def ring_chips(chips):
    half = chips // 2
    return [2 * p if p < half else 2 * (chips - 1 - p) + 1 for p in range(chips)]


def ring_pairs(chips):
    ring = ring_chips(chips)
    pairs = []
    for p in range(chips):
        pairs.append((2 * ring[p], 2 * ring[(p + 1) % chips]))
        pairs.append((2 * ring[p] + 1, 2 * ring[p - 1] + 1))
    return pairs


def chip_at(place, chips):
    place = lax.rem(place + 2 * chips, chips)
    return jnp.where(place < chips // 2, 2 * place, 2 * (chips - 1 - place) + 1)


def whereabouts(chips):
    blk = lax.axis_index("blk")
    chip, core = blk // 2, lax.rem(blk, 2)
    z = chip // 2
    place = jnp.where(lax.rem(chip, 2) == 0, z, chips - 1 - z)
    return chip, core, place


def pair_slots(chips):
    _, core, place = whereabouts(chips)
    sign = 1 - 2 * core
    slots = [(chip_at(place, chips), core)]
    for step in range(1, chips // 2):
        slots.append((chip_at(place - step * sign, chips), core))
        slots.append((chip_at(place + step * sign, chips), 1 - core))
    slots.append((chip_at(place + chips // 2, chips), core))
    return slots


def swapped(row, swap):
    half = row.shape[1] // 2
    other = jnp.concatenate([row[:, half:], row[:, :half]], axis=1)
    return jnp.where(swap == 1, other, row)


def merge_parts(messages):
    n = messages[0].shape[0] // 3
    tops = [m[:n] for m in messages]
    top = functools.reduce(jnp.maximum, tops)
    total = sum(m[n : 2 * n] * jnp.exp(t - top) for m, t in zip(messages, tops))
    return top, total, functools.reduce(jnp.maximum, [m[2 * n :] for m in messages])


def hold_kernel(chips, pieces, w_hbm, pair_hbm, labels_hbm, offset_ref, *refs):
    w_ref, _, x_ref, _, msg_ref, labels_ref, sem, pair_sem, label_sem = refs
    rows = w_ref.shape[0] // pieces
    copies = [
        pltpu.make_async_copy(
            w_hbm.at[pl.ds(i * rows, rows)], w_ref.at[pl.ds(i * rows, rows)], sem.at[i]
        )
        for i in range(pieces)
    ]
    label_copy = pltpu.make_async_copy(labels_hbm, labels_ref, label_sem)
    label_copy.start()
    pair_copy = pltpu.make_async_copy(
        pair_hbm, x_ref.at[pl.ds(0, pair_hbm.shape[0])], pair_sem
    )
    pair_copy.start()
    for copy in copies:
        copy.start()
    label_copy.wait()
    msg_ref[: 2 * chips] = jnp.zeros((2 * chips, LANES), f32)
    msg_ref[2 * chips :] = jnp.full((chips, LANES), NO_LABEL, f32)
    mine = (labels_ref[...] - offset_ref[0]).astype(f32)
    none = jnp.full_like(mine, NO_LABEL)
    chip, core, _ = whereabouts(chips)
    msg_ref[pl.ds(2 * chips + chip, 1), :] = jnp.concatenate(
        [jnp.where(core == 0, mine, none), jnp.where(core == 0, none, mine)], axis=1
    )
    for copy in copies:
        copy.wait()
    pair_copy.wait()


def hold(weight, pair, labels, offset, chips, batch, held_rows):
    pieces = 4
    rows, feats = weight.shape
    labels = labels.reshape(1, -1)
    return pl.pallas_call(
        functools.partial(hold_kernel, chips, pieces),
        name="hold_weight",
        out_shape=[
            pltpu.VMEM((rows, feats), bf16),
            pltpu.VMEM((rows, batch), f32),
            pltpu.VMEM((batch, feats), bf16),
            pltpu.VMEM((held_rows, feats), f32),
            pltpu.VMEM((3 * chips, LANES), f32),
        ],
        in_specs=[ANY, ANY, ANY, SM],
        out_specs=[VM] * 5,
        scratch_shapes=[
            pltpu.VMEM(labels.shape, i32),
            pltpu.SemaphoreType.DMA((pieces,)),
            pltpu.SemaphoreType.DMA,
            pltpu.SemaphoreType.DMA,
        ],
        compiler_params=pltpu.CompilerParams(vmem_limit_bytes=SCOPED),
        cost_estimate=pl.CostEstimate(
            flops=0, bytes_accessed=weight.size * 2, transcendentals=0
        ),
    )(in_hbm(weight), in_hbm(pair), in_hbm(labels), offset)


def fold(op, values):
    return op(values.reshape(values.shape[0] // 8, 8, values.shape[1]), axis=0)


def more_stats(logits, top, total):
    new_top = jnp.maximum(top, fold(jnp.max, logits))
    terms = jnp.exp(logits.reshape(logits.shape[0] // 8, 8, logits.shape[1]) - new_top[None])
    return new_top, total * jnp.exp(top - new_top) + jnp.sum(terms, axis=0)


def score_kernel(cfg, *refs):
    chips, k, held, bm, n_blocks = cfg
    blocks, accum_hbm, refs = refs[:n_blocks], refs[n_blocks], refs[n_blocks + 1 :]
    msg_in, refs = refs[0], refs[5:]
    msg_ref, w_ref, logits_ref, x_ref, acc_ref, acc_sem, x_sem = refs
    rows, width = w_ref.shape[0], 2 * LANES
    columns = pl.ds(k * width, width)
    if k == 0:
        copy = pltpu.make_async_copy(blocks[0], x_ref.at[pl.ds(LANES, LANES)], x_sem)
        copy.start()
    accum_copy = None
    if held[1] > held[0]:
        part = pl.ds(held[0], held[1] - held[0])
        accum_copy = pltpu.make_async_copy(accum_hbm.at[part], acc_ref.at[part], acc_sem)

        def start(_, carry):
            accum_copy.start()
            return carry

        lax.fori_loop(0, jnp.minimum(lax.axis_index("blk") + 1, 1), start, 0)
    if k == 0:
        copy.wait()
    else:
        at = k * width
        for block in blocks:
            x_ref[pl.ds(at, block.shape[0]), :] = block[...]
            at += block.shape[0]
    x = x_ref.at[columns]
    top = jnp.full((8, width), -3.0e38, f32)
    total = jnp.zeros((8, width), f32)
    for i in range(rows // bm):
        logits_ref[pl.ds(i * bm, bm), columns] = lax.dot_general(
            w_ref[pl.ds(i * bm, bm), :],
            x[...],
            (((1,), (1,)), ((), ())),
            preferred_element_type=f32,
        )
        if i > 0:
            top, total = more_stats(logits_ref[pl.ds((i - 1) * bm, bm), columns], top, total)
    top, total = more_stats(logits_ref[pl.ds(rows - bm, bm), columns], top, total)
    one_top = jnp.max(top, axis=0, keepdims=True)
    one_total = jnp.sum(total * jnp.exp(top - one_top), axis=0, keepdims=True)
    msg_ref[...] = msg_in[...]
    slots = pair_slots(chips)[2 * k : 2 * k + 2]
    for j, (owner, swap) in enumerate(slots):
        lanes = slice(j * LANES, (j + 1) * LANES)
        msg_ref[pl.ds(owner, 1), :] = swapped(one_top[:, lanes], swap)
        msg_ref[pl.ds(chips + owner, 1), :] = swapped(one_total[:, lanes], swap)
    if accum_copy is not None:
        accum_copy.wait()


def score(k, chips, blocks, accum, held, state):
    rows, feats = state[1].shape
    bm = min(512, rows)
    width = 2 * LANES
    base = len(blocks) + 2
    place = in_hbm if k == 0 else in_vmem
    inputs = [place(b) for b in blocks] + [in_hbm(accum)] + [in_vmem(s) for s in state]
    specs = [ANY if k == 0 else VM] * len(blocks) + [ANY]
    aliases = {base + i: 1 + i for i in range(4)}
    specs += [VM] * (len(inputs) - len(specs))
    cfg = (chips, k, held, bm, len(blocks))
    return pl.pallas_call(
        functools.partial(score_kernel, cfg),
        name=f"score_{k}",
        out_shape=[pltpu.VMEM(a.shape, a.dtype) for a in state],
        in_specs=specs,
        out_specs=[VM] * 5,
        input_output_aliases=aliases,
        scratch_shapes=[pltpu.SemaphoreType.DMA, pltpu.SemaphoreType.DMA],
        compiler_params=pltpu.CompilerParams(vmem_limit_bytes=SCOPED),
        cost_estimate=pl.CostEstimate(
            flops=2 * rows * feats * width,
            bytes_accessed=(rows + width) * feats * 2,
            transcendentals=rows * width,
        ),
    )(*inputs)


def small_call(kernel, name, shape, inputs, pinned):
    n = len(inputs)

    def with_pinned(*refs):
        kernel(*refs[:n], refs[n + len(pinned)])

    out, *pinned = pl.pallas_call(
        with_pinned,
        name=name,
        out_shape=[pltpu.VMEM(shape, inputs[0].dtype)]
        + [pltpu.VMEM(p.shape, p.dtype) for p in pinned],
        in_specs=[VM] * (n + len(pinned)),
        out_specs=[VM] * (1 + len(pinned)),
        input_output_aliases={n + i: 1 + i for i in range(len(pinned))},
        compiler_params=pltpu.CompilerParams(vmem_limit_bytes=SCOPED),
    )(*[in_vmem(a) for a in [*inputs, *pinned]])
    return out, pinned


def head_kernel(x_ref, out_ref):
    out_ref[...] = x_ref[: out_ref.shape[0], :]


def merge_kernel(*refs):
    top, total, labels = merge_parts([r[...] for r in refs[:-1]])
    n = top.shape[0]
    refs[-1][:n] = top
    refs[-1][n : 2 * n] = total
    refs[-1][2 * n :] = labels


def update_kernel(cfg, *refs):
    chips, n_msgs, bm, held_blocks, bn = cfg
    msgs, refs = refs[:n_msgs], refs[n_msgs:]
    other_ref, accum_hbm, logits_ref, x_ref = refs[:4]
    w_ref, acc_ref, out_w, out_acc, out_lse = refs[6:11]
    canon_s, lse_s, label_s, delta_s, grad_s, read_sem, acc_sem, w_sem = refs[11:]
    rows, batch = logits_ref.shape
    feats = x_ref.shape[1]
    blocks = rows // bm

    chip, core, _ = whereabouts(chips)
    rank = lax.axis_index("blk") * lax.axis_size("cls") + lax.axis_index("cls")
    first_class = rank * rows
    top, total, labels = merge_parts([m[...] for m in msgs])
    slab_lse = top + jnp.log(total)
    other = other_ref[...]
    high = jnp.maximum(slab_lse, other)
    lse = high + jnp.log(jnp.exp(slab_lse - high) + jnp.exp(other - high))
    canon_s[:chips] = lse
    canon_s[chips:] = labels
    own = canon_s[pl.ds(chip, 1), :]
    out_lse[...] = jnp.where(core == 0, own[:, : LANES // 2], own[:, LANES // 2 :])
    for j, (owner, swap) in enumerate(pair_slots(chips)):
        lanes = pl.ds(j * LANES, LANES)
        lse_s[:, lanes] = swapped(canon_s[pl.ds(owner, 1), :], swap)
        label_s[:, lanes] = (
            swapped(canon_s[pl.ds(chips + owner, 1), :], swap).astype(i32) - first_class
        )

    def make_delta(i, to):
        r0 = pl.multiple_of(i * bm, bm)
        chance = jnp.exp(logits_ref[pl.ds(r0, bm), :] - lse_s[...])
        row = lax.broadcasted_iota(i32, (bm, batch), 0)
        hit = row == (label_s[...] - r0)
        delta_s[to] = jnp.where(hit, chance - 1.0, chance).astype(bf16)

    def rows_of(i):
        return pl.ds(pl.multiple_of(i * bm, bm), bm)

    def read(i):
        slot = lax.rem(i, held_blocks)
        return pltpu.make_async_copy(
            accum_hbm.at[rows_of(i)], acc_ref.at[rows_of(slot)], read_sem.at[slot]
        )

    def writes(i):
        slot = lax.rem(i, held_blocks)
        return (
            pltpu.make_async_copy(
                acc_ref.at[rows_of(slot)], out_acc.at[rows_of(i)], acc_sem.at[slot]
            ),
            pltpu.make_async_copy(
                w_ref.at[rows_of(i)], out_w.at[rows_of(i)], w_sem.at[lax.rem(i, LAG + 1)]
            ),
        )

    make_delta(0, 0)

    def step(i, carry):
        now = lax.rem(i, 2)
        slot = lax.rem(i, held_blocks)

        @pl.when(i >= held_blocks)
        def _():
            read(i).wait()

        make_delta(jnp.minimum(i + 1, blocks - 1), 1 - now)
        def grad_tile(n):
            grad_s[n % 2] = jnp.dot(
                delta_s[now], x_ref[:, pl.ds(n * bn, bn)], preferred_element_type=f32
            )

        def update_tile(n):
            cols = pl.ds(n * bn, bn)
            for r in range(0, bm, SUB):
                a_rows = pl.ds(pl.multiple_of(slot * bm + r, SUB), SUB)
                w_rows = pl.ds(pl.multiple_of(i * bm + r, SUB), SUB)
                grad = grad_s[n % 2, pl.ds(r, SUB), :]
                new_acc = acc_ref[a_rows, cols] + grad * grad
                acc_ref[a_rows, cols] = new_acc
                root = new_acc * lax.rsqrt(new_acc)
                part = (0.05 * grad) * pltpu.reciprocal(root + 1e-10, approx=True)
                w_ref[w_rows, cols] = (w_ref[w_rows, cols].astype(f32) - part).astype(bf16)

        tiles = feats // bn
        grad_tile(0)
        for n in range(1, tiles):
            grad_tile(n)
            update_tile(n - 1)
        update_tile(tiles - 1)

        @pl.when(i >= LAG)
        def _():
            for copy in writes(i - LAG):
                copy.wait()

            @pl.when(i - LAG + held_blocks < blocks)
            def _():
                read(i - LAG + held_blocks).start()

        for copy in writes(i):
            copy.start()
        return carry

    lax.fori_loop(0, blocks, step, 0)
    for i in range(max(0, blocks - LAG), blocks):
        for copy in writes(i):
            copy.wait()


def update(chips, msgs, other, accum, logits, x, weight_v, acc_v, bm):
    rows, batch = logits.shape
    feats = x.shape[1]
    held_blocks = acc_v.shape[0] // bm
    bn = min(256, feats)
    inputs = [in_vmem(m) for m in msgs] + [other, in_hbm(accum)] + [
        in_vmem(a) for a in (logits, x, weight_v, acc_v)
    ]
    n = len(msgs)
    cfg = (chips, n, bm, held_blocks, bn)
    outs = pl.pallas_call(
        functools.partial(update_kernel, cfg),
        name="update",
        out_shape=[
            pltpu.VMEM(weight_v.shape, bf16),
            pltpu.VMEM(acc_v.shape, f32),
            pltpu.HBM((rows, feats), bf16),
            pltpu.HBM((rows, feats), f32),
            jax.ShapeDtypeStruct((1, LANES // 2), f32),
        ],
        in_specs=[VM] * n + [VM, ANY, VM, VM, VM, VM],
        out_specs=[VM, VM, ANY, ANY, VM],
        input_output_aliases={n + 4: 0, n + 5: 1},
        scratch_shapes=[
            pltpu.VMEM((2 * chips, LANES), f32),
            pltpu.VMEM((1, batch), f32),
            pltpu.VMEM((1, batch), i32),
            pltpu.VMEM((2, bm, batch), bf16),
            pltpu.VMEM((2, bm, bn), f32),
            pltpu.SemaphoreType.DMA((held_blocks,)),
            pltpu.SemaphoreType.DMA((held_blocks,)),
            pltpu.SemaphoreType.DMA((LAG + 1,)),
        ],
        compiler_params=pltpu.CompilerParams(vmem_limit_bytes=SCOPED),
        cost_estimate=pl.CostEstimate(
            flops=2 * rows * feats * batch,
            bytes_accessed=rows * feats * 10,
            transcendentals=rows * batch,
        ),
    )(*inputs)
    return outs[2:]


def exchange_stats(message, pinned, blk_size, cls_size):
    bits_cls = cls_size.bit_length() - 1
    bits = bits_cls + blk_size.bit_length() - 1
    core, y = bits_cls, bits_cls + 1
    rest = [b for b in range(bits) if b not in (core, y, 0)]
    groups = [(core,), (0, y)] + [tuple(rest[i : i + 2]) for i in range(0, len(rest), 2)]
    messages = [message]
    for group in groups:
        if len(messages) > 1:
            message, pinned = small_call(
                merge_kernel, "merge_stats", message.shape, messages, pinned
            )
        messages = [message]
        for pick in range(1, 2 ** len(group)):
            flip = sum(1 << b for at, b in enumerate(group) if pick >> at & 1)
            pairs = [(d, d ^ flip) for d in range(blk_size * cls_size)]
            messages.append(lax.ppermute(message, ("blk", "cls"), pairs))
    return messages, pinned


def body(features, labels, offset, other_lse, weight, accum):
    blk_size, cls_size = lax.axis_size("blk"), lax.axis_size("cls")
    chips = blk_size // 2
    steps = chips // 2
    block, feats = features.shape
    rows = weight.shape[0]
    batch = block * blk_size
    bm = min(256 * 1024 // batch, rows)
    held_rows = min(rows, HELD_BYTES // (feats * 4))

    def swap_cores(x):
        return lax.ppermute(x, "blk", [(d, d ^ 1) for d in range(blk_size)])

    def round_ring(x):
        return lax.ppermute(x, "blk", ring_pairs(chips))

    sibling = swap_cores(features)
    pair = jnp.concatenate([features, sibling], axis=0)
    came = round_ring(pair)
    *pinned, message = hold(weight, pair, labels, offset, chips, batch, held_rows)
    state = [message, *pinned]
    came, state[0] = lax.optimization_barrier((came, state[0]))
    blocks = [came]
    for k in range(steps):
        if k < steps - 1:
            crossed = swap_cores(came)
            if k == steps - 2:
                came, state[1:] = small_call(head_kernel, "head", (block, feats), [came], state[1:])
            came = round_ring(came)
        cut = [bm * min(held_rows // bm, 4 * i) for i in (k, k + 1)]
        state = list(score(k, chips, blocks, accum, tuple(cut), state))
        if k < steps - 1:
            came, state[0] = lax.optimization_barrier((came, state[0]))
            blocks = [crossed, came] + ([swap_cores(came)] if k == steps - 2 else [])
    messages, pinned = exchange_stats(state[0], state[1:], blk_size, cls_size)
    weight_v, logits, x, acc_v = pinned
    new_weight, new_accum, lse = update(
        chips, messages, other_lse.reshape(chips, LANES), accum, logits, x, weight_v, acc_v, bm
    )
    return (new_weight, new_accum, lse.reshape(block))


def solution(mesh):
    in_specs = (
        P("blk", None),
        P("blk"),
        P(),
        P(),
        P(("blk", "cls"), None),
        P(("blk", "cls"), None),
    )
    out_specs = (P(("blk", "cls"), None), P(("blk", "cls"), None), P("blk"))
    return jax.shard_map(body, mesh=mesh, in_specs=in_specs, out_specs=out_specs, check_vma=False)
```

```python
import functools

import jax
import jax.numpy as jnp
from jax import lax
from jax.experimental import pallas as pl
from jax.experimental.pallas import tpu as pltpu
from jax.sharding import PartitionSpec as P

f32, bf16, i32 = jnp.float32, jnp.bfloat16, jnp.int32
VM = pl.BlockSpec(memory_space=pltpu.VMEM)
ANY = pl.BlockSpec(memory_space=pl.ANY)
SM = pl.BlockSpec(memory_space=pltpu.SMEM)
MIB = 2**20
LANES = 128
PIECES = 2
HELD_BYTES = 20 * MIB
SUB = 32
LAG = 2
NO_LABEL = -4.0e6
SCOPED = 4 * MIB


def in_vmem(x):
    return pltpu.with_memory_space_constraint(x, pltpu.VMEM)


def in_hbm(x):
    return pltpu.with_memory_space_constraint(x, pltpu.HBM)


def ring_chips(chips):
    half = chips // 2
    return [2 * p if p < half else 2 * (chips - 1 - p) + 1 for p in range(chips)]


def ring_pairs(chips):
    ring = ring_chips(chips)
    pairs = []
    for p in range(chips):
        pairs.append((2 * ring[p], 2 * ring[(p + 1) % chips]))
        pairs.append((2 * ring[p] + 1, 2 * ring[p - 1] + 1))
    return pairs


def chip_at(place, chips):
    place = lax.rem(place + 2 * chips, chips)
    return jnp.where(place < chips // 2, 2 * place, 2 * (chips - 1 - place) + 1)


def whereabouts(chips):
    blk = lax.axis_index("blk")
    chip, core = blk // 2, lax.rem(blk, 2)
    z = chip // 2
    place = jnp.where(lax.rem(chip, 2) == 0, z, chips - 1 - z)
    return chip, core, place


def block_slots(chips):
    _, core, place = whereabouts(chips)
    sign = 1 - 2 * core
    slots = [(place, core), (place, 1 - core), (place - sign, core), (place + sign, 1 - core)]
    for step in range(2, chips // 2 + 1):
        near, far = (step - 1) * sign, step * sign
        slots += [(place - near, 1 - core), (place - far, core)]
        slots += [(place + near, core), (place + far, 1 - core)]
    return [(chip_at(at, chips), side) for at, side in slots]


def one_half(row, side):
    half = row.shape[1] // 2
    return jnp.where(side == 0, row[:, :half], row[:, half:])


def merge_parts(messages):
    n = messages[0].shape[0] // 3
    tops = [m[:n] for m in messages]
    top = functools.reduce(jnp.maximum, tops)
    total = sum(m[n : 2 * n] * jnp.exp(t - top) for m, t in zip(messages, tops))
    return top, total, functools.reduce(jnp.maximum, [m[2 * n :] for m in messages])


def weight_copies(w_hbm, w_ref, sem, half):
    pieces = sem.shape[0]
    rows = w_ref.shape[0] // 2 // pieces
    first = half * pieces
    return [
        pltpu.make_async_copy(
            w_hbm.at[pl.ds((first + i) * rows, rows)],
            w_ref.at[pl.ds((first + i) * rows, rows)],
            sem.at[i],
        )
        for i in range(pieces)
    ]


def hold_kernel(chips, w_hbm, labels_hbm, offset_ref, *refs):
    w_ref, _, _, _, msg_ref, labels_ref, sem, label_sem = refs
    copies = weight_copies(w_hbm, w_ref, sem, 0)
    label_copy = pltpu.make_async_copy(labels_hbm, labels_ref, label_sem)
    label_copy.start()
    for copy in copies:
        copy.start()
    label_copy.wait()
    msg_ref[: 2 * chips] = jnp.zeros((2 * chips, LANES), f32)
    msg_ref[2 * chips :] = jnp.full((chips, LANES), NO_LABEL, f32)
    mine = (labels_ref[...] - offset_ref[0]).astype(f32)
    none = jnp.full_like(mine, NO_LABEL)
    chip, core, _ = whereabouts(chips)
    msg_ref[pl.ds(2 * chips + chip, 1), :] = jnp.concatenate(
        [jnp.where(core == 0, mine, none), jnp.where(core == 0, none, mine)], axis=1
    )
    for copy in copies:
        copy.wait()


def hold(weight, labels, offset, chips, batch, held_rows):
    rows, feats = weight.shape
    labels = labels.reshape(1, -1)
    return pl.pallas_call(
        functools.partial(hold_kernel, chips),
        name="hold_weight",
        out_shape=[
            pltpu.VMEM((rows, feats), bf16),
            pltpu.VMEM((rows, batch), f32),
            pltpu.VMEM((batch, feats), bf16),
            pltpu.VMEM((held_rows, feats), f32),
            pltpu.VMEM((3 * chips, LANES), f32),
        ],
        in_specs=[ANY, ANY, SM],
        out_specs=[VM] * 5,
        scratch_shapes=[
            pltpu.VMEM(labels.shape, i32),
            pltpu.SemaphoreType.DMA((PIECES,)),
            pltpu.SemaphoreType.DMA,
        ],
        compiler_params=pltpu.CompilerParams(vmem_limit_bytes=SCOPED),
        cost_estimate=pl.CostEstimate(
            flops=0, bytes_accessed=weight.size, transcendentals=0
        ),
    )(in_hbm(weight), in_hbm(labels), offset)


def fold(op, values):
    return op(values.reshape(values.shape[0] // 8, 8, values.shape[1]), axis=0)


def more_stats(logits, top, total):
    new_top = jnp.maximum(top, fold(jnp.max, logits))
    terms = jnp.exp(logits.reshape(logits.shape[0] // 8, 8, logits.shape[1]) - new_top[None])
    return new_top, total * jnp.exp(top - new_top) + jnp.sum(terms, axis=0)


def score_kernel(cfg, *refs):
    chips, k, held, bm, n_blocks = cfg
    blocks, accum_hbm, w_hbm, refs = refs[:n_blocks], refs[n_blocks], refs[n_blocks + 1], refs[n_blocks + 2 :]
    msg_in, refs = refs[0], refs[5:]
    msg_ref, w_ref, logits_ref, x_ref, acc_ref, acc_sem, w_sem = refs
    rows, width = w_ref.shape[0], 2 * LANES
    columns = pl.ds(k * width, width)
    copies = weight_copies(w_hbm, w_ref, w_sem, 1) if k == 0 else []
    accum_copies = []
    if held[1] > held[0]:
        part = pl.ds(held[0], held[1] - held[0])
        accum_copies = [pltpu.make_async_copy(accum_hbm.at[part], acc_ref.at[part], acc_sem)]

    def start(_, carry):
        for copy in copies + accum_copies:
            copy.start()
        return carry

    if copies + accum_copies:
        lax.fori_loop(0, jnp.minimum(lax.axis_index("blk") + 1, 1), start, 0)
    at = k * width
    for block in blocks:
        x_ref[pl.ds(at, block.shape[0]), :] = block[...]
        at += block.shape[0]
    x = x_ref.at[columns]
    top = jnp.full((8, width), -3.0e38, f32)
    total = jnp.zeros((8, width), f32)
    for i in range(rows // bm):
        if i == rows // bm // 2:
            for copy in copies:
                copy.wait()
        logits_ref[pl.ds(i * bm, bm), columns] = lax.dot_general(
            w_ref[pl.ds(i * bm, bm), :],
            x[...],
            (((1,), (1,)), ((), ())),
            preferred_element_type=f32,
        )
        if i > 0:
            top, total = more_stats(logits_ref[pl.ds((i - 1) * bm, bm), columns], top, total)
    top, total = more_stats(logits_ref[pl.ds(rows - bm, bm), columns], top, total)
    one_top = jnp.max(top, axis=0, keepdims=True)
    one_total = jnp.sum(total * jnp.exp(top - one_top), axis=0, keepdims=True)
    msg_ref[...] = msg_in[...]
    half = LANES // 2
    side_of = lax.broadcasted_iota(i32, (1, LANES), 1) // half
    for j, (owner, side) in enumerate(block_slots(chips)[4 * k : 4 * k + 4]):
        lanes = slice(j * half, (j + 1) * half)
        for row, values in ((owner, one_top), (chips + owner, one_total)):
            twice = jnp.concatenate([values[:, lanes], values[:, lanes]], axis=1)
            here = pl.ds(row, 1)
            msg_ref[here, :] = jnp.where(side_of == side, twice, msg_ref[here, :])
    for copy in accum_copies:
        copy.wait()


def score(k, chips, blocks, accum, weight, held, state):
    rows, feats = state[1].shape
    bm = min(512, rows // 2)
    width = 2 * LANES
    base = len(blocks) + 3
    inputs = [in_vmem(b) for b in blocks] + [in_hbm(accum), in_hbm(weight)]
    inputs += [in_vmem(s) for s in state]
    specs = [VM] * len(blocks) + [ANY, ANY] + [VM] * len(state)
    aliases = {base + i: 1 + i for i in range(4)}
    cfg = (chips, k, held, bm, len(blocks))
    return pl.pallas_call(
        functools.partial(score_kernel, cfg),
        name=f"score_{k}",
        out_shape=[pltpu.VMEM(a.shape, a.dtype) for a in state],
        in_specs=specs,
        out_specs=[VM] * 5,
        input_output_aliases=aliases,
        scratch_shapes=[pltpu.SemaphoreType.DMA, pltpu.SemaphoreType.DMA((PIECES,))],
        compiler_params=pltpu.CompilerParams(vmem_limit_bytes=SCOPED),
        cost_estimate=pl.CostEstimate(
            flops=2 * rows * feats * width,
            bytes_accessed=(rows + width) * feats * 2,
            transcendentals=rows * width,
        ),
    )(*inputs)


def small_call(kernel, name, shape, inputs, pinned):
    n = len(inputs)

    def with_pinned(*refs):
        kernel(*refs[:n], refs[n + len(pinned)])

    out, *pinned = pl.pallas_call(
        with_pinned,
        name=name,
        out_shape=[pltpu.VMEM(shape, inputs[0].dtype)]
        + [pltpu.VMEM(p.shape, p.dtype) for p in pinned],
        in_specs=[VM] * (n + len(pinned)),
        out_specs=[VM] * (1 + len(pinned)),
        input_output_aliases={n + i: 1 + i for i in range(len(pinned))},
        compiler_params=pltpu.CompilerParams(vmem_limit_bytes=SCOPED),
    )(*[in_vmem(a) for a in [*inputs, *pinned]])
    return out, pinned


def join_kernel(first_ref, second_ref, out_ref):
    n = first_ref.shape[0]
    out_ref[:n] = first_ref[...]
    out_ref[n:] = second_ref[...]


def merge_kernel(*refs):
    top, total, labels = merge_parts([r[...] for r in refs[:-1]])
    n = top.shape[0]
    refs[-1][:n] = top
    refs[-1][n : 2 * n] = total
    refs[-1][2 * n :] = labels


def update_kernel(cfg, *refs):
    chips, n_msgs, bm, held_blocks, bn = cfg
    msgs, refs = refs[:n_msgs], refs[n_msgs:]
    other_ref, accum_hbm, logits_ref, x_ref = refs[:4]
    w_ref, acc_ref, out_w, out_acc, out_lse = refs[6:11]
    canon_s, lse_s, label_s, delta_s, grad_s, read_sem, acc_sem, w_sem = refs[11:]
    rows, batch = logits_ref.shape
    feats = x_ref.shape[1]
    blocks = rows // bm

    chip, core, _ = whereabouts(chips)
    rank = lax.axis_index("blk") * lax.axis_size("cls") + lax.axis_index("cls")
    first_class = rank * rows
    top, total, labels = merge_parts([m[...] for m in msgs])
    slab_lse = top + jnp.log(total)
    other = other_ref[...]
    high = jnp.maximum(slab_lse, other)
    lse = high + jnp.log(jnp.exp(slab_lse - high) + jnp.exp(other - high))
    canon_s[:chips] = lse
    canon_s[chips:] = labels
    own = canon_s[pl.ds(chip, 1), :]
    out_lse[...] = jnp.where(core == 0, own[:, : LANES // 2], own[:, LANES // 2 :])
    slots = block_slots(chips)
    for j in range(chips):
        lanes = pl.ds(j * LANES, LANES)
        pair = slots[2 * j : 2 * j + 2]
        lse_s[:, lanes] = jnp.concatenate(
            [one_half(canon_s[pl.ds(owner, 1), :], side) for owner, side in pair], axis=1
        )
        label = jnp.concatenate(
            [one_half(canon_s[pl.ds(chips + owner, 1), :], side) for owner, side in pair], axis=1
        )
        label_s[:, lanes] = label.astype(i32) - first_class

    def make_delta(i, to):
        r0 = pl.multiple_of(i * bm, bm)
        chance = jnp.exp(logits_ref[pl.ds(r0, bm), :] - lse_s[...])
        row = lax.broadcasted_iota(i32, (bm, batch), 0)
        hit = row == (label_s[...] - r0)
        delta_s[to] = jnp.where(hit, chance - 1.0, chance).astype(bf16)

    def rows_of(i):
        return pl.ds(pl.multiple_of(i * bm, bm), bm)

    def read(i):
        slot = lax.rem(i, held_blocks)
        return pltpu.make_async_copy(
            accum_hbm.at[rows_of(i)], acc_ref.at[rows_of(slot)], read_sem.at[slot]
        )

    def writes(i):
        slot = lax.rem(i, held_blocks)
        return (
            pltpu.make_async_copy(
                acc_ref.at[rows_of(slot)], out_acc.at[rows_of(i)], acc_sem.at[slot]
            ),
            pltpu.make_async_copy(
                w_ref.at[rows_of(i)], out_w.at[rows_of(i)], w_sem.at[lax.rem(i, LAG + 1)]
            ),
        )

    make_delta(0, 0)
    grad_s[...] = jnp.zeros_like(grad_s)

    def step(i, carry):
        now = lax.rem(i, 2)
        slot = lax.rem(i, held_blocks)

        @pl.when(i >= held_blocks)
        def _():
            read(i).wait()

        make_delta(jnp.minimum(i + 1, blocks - 1), 1 - now)
        def grad_tile(n):
            grad_s[n % 2] = jnp.dot(
                delta_s[now], x_ref[:, pl.ds(n * bn, bn)], preferred_element_type=f32
            )

        def update_tile(n):
            cols = pl.ds(n * bn, bn)
            for r in range(0, bm, SUB):
                a_rows = pl.ds(pl.multiple_of(slot * bm + r, SUB), SUB)
                w_rows = pl.ds(pl.multiple_of(i * bm + r, SUB), SUB)
                grad = grad_s[n % 2, pl.ds(r, SUB), :]
                new_acc = acc_ref[a_rows, cols] + grad * grad
                acc_ref[a_rows, cols] = new_acc
                root = new_acc * lax.rsqrt(new_acc)
                part = (0.05 * grad) * pltpu.reciprocal(root + 1e-10, approx=True)
                w_ref[w_rows, cols] = (w_ref[w_rows, cols].astype(f32) - part).astype(bf16)

        tiles = feats // bn
        grad_tile(0)
        for n in range(1, tiles):
            grad_tile(n)
            update_tile(n - 1)
        update_tile(tiles - 1)

        @pl.when(i >= LAG)
        def _():
            for copy in writes(i - LAG):
                copy.wait()

            @pl.when(i - LAG + held_blocks < blocks)
            def _():
                read(i - LAG + held_blocks).start()

        for copy in writes(i):
            copy.start()
        return carry

    lax.fori_loop(0, blocks, step, 0)
    for i in range(max(0, blocks - LAG), blocks):
        for copy in writes(i):
            copy.wait()


def update(chips, msgs, other, accum, logits, x, weight_v, acc_v, bm):
    rows, batch = logits.shape
    feats = x.shape[1]
    held_blocks = acc_v.shape[0] // bm
    bn = min(256, feats)
    inputs = [in_vmem(m) for m in msgs] + [other, in_hbm(accum)] + [
        in_vmem(a) for a in (logits, x, weight_v, acc_v)
    ]
    n = len(msgs)
    cfg = (chips, n, bm, held_blocks, bn)
    outs = pl.pallas_call(
        functools.partial(update_kernel, cfg),
        name="update",
        out_shape=[
            pltpu.VMEM(weight_v.shape, bf16),
            pltpu.VMEM(acc_v.shape, f32),
            pltpu.HBM((rows, feats), bf16),
            pltpu.HBM((rows, feats), f32),
            jax.ShapeDtypeStruct((1, LANES // 2), f32),
        ],
        in_specs=[VM] * n + [VM, ANY, VM, VM, VM, VM],
        out_specs=[VM, VM, ANY, ANY, VM],
        input_output_aliases={n + 4: 0, n + 5: 1},
        scratch_shapes=[
            pltpu.VMEM((2 * chips, LANES), f32),
            pltpu.VMEM((1, batch), f32),
            pltpu.VMEM((1, batch), i32),
            pltpu.VMEM((2, bm, batch), bf16),
            pltpu.VMEM((2, bm, bn), f32),
            pltpu.SemaphoreType.DMA((held_blocks,)),
            pltpu.SemaphoreType.DMA((held_blocks,)),
            pltpu.SemaphoreType.DMA((LAG + 1,)),
        ],
        compiler_params=pltpu.CompilerParams(vmem_limit_bytes=SCOPED),
        cost_estimate=pl.CostEstimate(
            flops=2 * rows * feats * batch,
            bytes_accessed=rows * feats * 10,
            transcendentals=rows * batch,
        ),
    )(*inputs)
    return outs[2:]


def exchange_stats(message, pinned, blk_size, cls_size):
    bits_cls = cls_size.bit_length() - 1
    bits = bits_cls + blk_size.bit_length() - 1
    core, y = bits_cls, bits_cls + 1
    rest = [b for b in range(bits) if b not in (core, y, 0)]
    groups = [(core,), (0, y)] + [tuple(rest[i : i + 2]) for i in range(0, len(rest), 2)]
    messages = [message]
    for group in groups:
        if len(messages) > 1:
            message, pinned = small_call(
                merge_kernel, "merge_stats", message.shape, messages, pinned
            )
        messages = [message]
        for pick in range(1, 2 ** len(group)):
            flip = sum(1 << b for at, b in enumerate(group) if pick >> at & 1)
            pairs = [(d, d ^ flip) for d in range(blk_size * cls_size)]
            messages.append(lax.ppermute(message, ("blk", "cls"), pairs))
    return messages, pinned


def body(features, labels, offset, other_lse, weight, accum):
    blk_size, cls_size = lax.axis_size("blk"), lax.axis_size("cls")
    chips = blk_size // 2
    steps = chips // 2
    block, feats = features.shape
    rows = weight.shape[0]
    batch = block * blk_size
    bm = min(256 * 1024 // batch, rows)
    held_rows = min(rows, HELD_BYTES // (feats * 4))

    def swap_cores(x):
        return lax.ppermute(x, "blk", [(d, d ^ 1) for d in range(blk_size)])

    def round_ring(x):
        return lax.ppermute(x, "blk", ring_pairs(chips))

    came = round_ring(features)
    sibling = swap_cores(features)
    *pinned, message = hold(weight, labels, offset, chips, batch, held_rows)
    came, message = lax.optimization_barrier((came, message))
    state = [message, *pinned]
    joined, state[1:] = small_call(
        join_kernel, "join", (2 * block, feats), [sibling, came], state[1:]
    )
    blocks = [features, sibling, came, swap_cores(came)]
    came = round_ring(joined)
    held = 0
    for k in range(steps):
        if k > 0:
            blocks = [came, swap_cores(came)]
            if k < steps - 1:
                came = round_ring(came)
        until = held_rows if k == steps - 1 else min(held_rows, 4 * k * bm)
        state = list(score(k, chips, blocks, accum, weight, (held, until), state))
        held = until
        if k < steps - 1:
            came, state[0] = lax.optimization_barrier((came, state[0]))
    messages, pinned = exchange_stats(state[0], state[1:], blk_size, cls_size)
    weight_v, logits, x, acc_v = pinned
    new_weight, new_accum, lse = update(
        chips, messages, other_lse.reshape(chips, LANES), accum, logits, x, weight_v, acc_v, bm
    )
    return (new_weight, new_accum, lse.reshape(block))


def solution(mesh):
    in_specs = (
        P("blk", None),
        P("blk"),
        P(),
        P(),
        P(("blk", "cls"), None),
        P(("blk", "cls"), None),
    )
    out_specs = (P(("blk", "cls"), None), P(("blk", "cls"), None), P("blk"))
    return jax.shard_map(body, mesh=mesh, in_specs=in_specs, out_specs=out_specs, check_vma=False)
```

```python
import functools

import jax
import jax.numpy as jnp
from jax import lax
from jax.experimental import pallas as pl
from jax.experimental.pallas import tpu as pltpu
from jax.sharding import PartitionSpec as P

f32, bf16, i32 = jnp.float32, jnp.bfloat16, jnp.int32
VM = pl.BlockSpec(memory_space=pltpu.VMEM)
ANY = pl.BlockSpec(memory_space=pl.ANY)
SM = pl.BlockSpec(memory_space=pltpu.SMEM)
MIB = 2**20
LANES = 128
PIECES = 2
HELD_BYTES = 20 * MIB
SUB = 32
LAG = 2
NO_LABEL = -4.0e6
SCOPED = 4 * MIB


def in_vmem(x):
    return pltpu.with_memory_space_constraint(x, pltpu.VMEM)


def in_hbm(x):
    return pltpu.with_memory_space_constraint(x, pltpu.HBM)


def ring_chips(chips):
    half = chips // 2
    return [2 * p if p < half else 2 * (chips - 1 - p) + 1 for p in range(chips)]


def ring_pairs(chips):
    ring = ring_chips(chips)
    pairs = []
    for p in range(chips):
        pairs.append((2 * ring[p], 2 * ring[(p + 1) % chips]))
        pairs.append((2 * ring[p] + 1, 2 * ring[p - 1] + 1))
    return pairs


def chip_at(place, chips):
    place = lax.rem(place + 2 * chips, chips)
    return jnp.where(place < chips // 2, 2 * place, 2 * (chips - 1 - place) + 1)


def whereabouts(chips):
    blk = lax.axis_index("blk")
    chip, core = blk // 2, lax.rem(blk, 2)
    z = chip // 2
    place = jnp.where(lax.rem(chip, 2) == 0, z, chips - 1 - z)
    return chip, core, place


def block_slots(chips):
    _, core, place = whereabouts(chips)
    sign = 1 - 2 * core
    slots = [(place, core), (place, 1 - core), (place - sign, core), (place + sign, 1 - core)]
    for step in range(2, chips // 2 + 1):
        near, far = (step - 1) * sign, step * sign
        slots += [(place - near, 1 - core), (place - far, core)]
        slots += [(place + near, core), (place + far, 1 - core)]
    return [(chip_at(at, chips), side) for at, side in slots]


def one_half(row, side):
    half = row.shape[1] // 2
    return jnp.where(side == 0, row[:, :half], row[:, half:])


def merge_parts(messages):
    n = messages[0].shape[0] // 3
    tops = [m[:n] for m in messages]
    top = functools.reduce(jnp.maximum, tops)
    total = sum(m[n : 2 * n] * jnp.exp(t - top) for m, t in zip(messages, tops))
    return top, total, functools.reduce(jnp.maximum, [m[2 * n :] for m in messages])


def weight_copies(w_hbm, w_ref, sem, half):
    pieces = sem.shape[0]
    rows = w_ref.shape[0] // 2 // pieces
    first = half * pieces
    return [
        pltpu.make_async_copy(
            w_hbm.at[pl.ds((first + i) * rows, rows)],
            w_ref.at[pl.ds((first + i) * rows, rows)],
            sem.at[i],
        )
        for i in range(pieces)
    ]


def hold_kernel(chips, w_hbm, labels_hbm, offset_ref, *refs):
    w_ref, _, _, _, msg_ref, labels_ref, sem, label_sem = refs
    copies = weight_copies(w_hbm, w_ref, sem, 0)
    label_copy = pltpu.make_async_copy(labels_hbm, labels_ref, label_sem)
    label_copy.start()
    for copy in copies:
        copy.start()
    label_copy.wait()
    msg_ref[: 2 * chips] = jnp.zeros((2 * chips, LANES), f32)
    msg_ref[2 * chips :] = jnp.full((chips, LANES), NO_LABEL, f32)
    mine = (labels_ref[...] - offset_ref[0]).astype(f32)
    none = jnp.full_like(mine, NO_LABEL)
    chip, core, _ = whereabouts(chips)
    msg_ref[pl.ds(2 * chips + chip, 1), :] = jnp.concatenate(
        [jnp.where(core == 0, mine, none), jnp.where(core == 0, none, mine)], axis=1
    )
    for copy in copies:
        copy.wait()


def hold(weight, labels, offset, chips, batch, held_rows):
    rows, feats = weight.shape
    labels = labels.reshape(1, -1)
    return pl.pallas_call(
        functools.partial(hold_kernel, chips),
        name="hold_weight",
        out_shape=[
            pltpu.VMEM((rows, feats), bf16),
            pltpu.VMEM((rows, batch), f32),
            pltpu.VMEM((batch, feats), bf16),
            pltpu.VMEM((held_rows, feats), f32),
            pltpu.VMEM((3 * chips, LANES), f32),
        ],
        in_specs=[ANY, ANY, SM],
        out_specs=[VM] * 5,
        scratch_shapes=[
            pltpu.VMEM(labels.shape, i32),
            pltpu.SemaphoreType.DMA((PIECES,)),
            pltpu.SemaphoreType.DMA,
        ],
        compiler_params=pltpu.CompilerParams(vmem_limit_bytes=SCOPED),
        cost_estimate=pl.CostEstimate(
            flops=0, bytes_accessed=weight.size, transcendentals=0
        ),
    )(in_hbm(weight), in_hbm(labels), offset)


def fold(op, values):
    return op(values.reshape(values.shape[0] // 8, 8, values.shape[1]), axis=0)


def more_stats(logits, top, total):
    new_top = jnp.maximum(top, fold(jnp.max, logits))
    terms = jnp.exp(logits.reshape(logits.shape[0] // 8, 8, logits.shape[1]) - new_top[None])
    return new_top, total * jnp.exp(top - new_top) + jnp.sum(terms, axis=0)


def score_kernel(cfg, *refs):
    chips, k, held, bm, n_blocks = cfg
    blocks, accum_hbm, w_hbm, refs = refs[:n_blocks], refs[n_blocks], refs[n_blocks + 1], refs[n_blocks + 2 :]
    msg_in, refs = refs[0], refs[5:]
    msg_ref, w_ref, logits_ref, x_ref, acc_ref, acc_sem, w_sem = refs
    rows, width = w_ref.shape[0], 2 * LANES
    columns = pl.ds(k * width, width)
    copies = weight_copies(w_hbm, w_ref, w_sem, 1) if k == 0 else []
    accum_copies = []
    if held[1] > held[0]:
        part = pl.ds(held[0], held[1] - held[0])
        accum_copies = [pltpu.make_async_copy(accum_hbm.at[part], acc_ref.at[part], acc_sem)]

    def start(_, carry):
        for copy in copies + accum_copies:
            copy.start()
        return carry

    if copies + accum_copies:
        lax.fori_loop(0, jnp.minimum(lax.axis_index("blk") + 1, 1), start, 0)
    at = k * width
    for block in blocks:
        x_ref[pl.ds(at, block.shape[0]), :] = block[...]
        at += block.shape[0]
    x = x_ref.at[columns]
    top = jnp.full((8, width), -3.0e38, f32)
    total = jnp.zeros((8, width), f32)
    for i in range(rows // bm):
        if i == rows // bm // 2:
            for copy in copies:
                copy.wait()
        logits_ref[pl.ds(i * bm, bm), columns] = lax.dot_general(
            w_ref[pl.ds(i * bm, bm), :],
            x[...],
            (((1,), (1,)), ((), ())),
            preferred_element_type=f32,
        )
        if i > 0:
            top, total = more_stats(logits_ref[pl.ds((i - 1) * bm, bm), columns], top, total)
    top, total = more_stats(logits_ref[pl.ds(rows - bm, bm), columns], top, total)
    one_top = jnp.max(top, axis=0, keepdims=True)
    one_total = jnp.sum(total * jnp.exp(top - one_top), axis=0, keepdims=True)
    msg_ref[...] = msg_in[...]
    half = LANES // 2
    side_of = lax.broadcasted_iota(i32, (1, LANES), 1) // half
    for j, (owner, side) in enumerate(block_slots(chips)[4 * k : 4 * k + 4]):
        lanes = slice(j * half, (j + 1) * half)
        for row, values in ((owner, one_top), (chips + owner, one_total)):
            twice = jnp.concatenate([values[:, lanes], values[:, lanes]], axis=1)
            here = pl.ds(row, 1)
            msg_ref[here, :] = jnp.where(side_of == side, twice, msg_ref[here, :])
    for copy in accum_copies:
        copy.wait()


def score(k, chips, blocks, accum, weight, held, state):
    rows, feats = state[1].shape
    bm = min(512, rows // 2)
    width = 2 * LANES
    base = len(blocks) + 3
    inputs = [in_vmem(b) for b in blocks] + [in_hbm(accum), in_hbm(weight)]
    inputs += [in_vmem(s) for s in state]
    specs = [VM] * len(blocks) + [ANY, ANY] + [VM] * len(state)
    aliases = {base + i: 1 + i for i in range(4)}
    cfg = (chips, k, held, bm, len(blocks))
    return pl.pallas_call(
        functools.partial(score_kernel, cfg),
        name=f"score_{k}",
        out_shape=[pltpu.VMEM(a.shape, a.dtype) for a in state],
        in_specs=specs,
        out_specs=[VM] * 5,
        input_output_aliases=aliases,
        scratch_shapes=[pltpu.SemaphoreType.DMA, pltpu.SemaphoreType.DMA((PIECES,))],
        compiler_params=pltpu.CompilerParams(vmem_limit_bytes=SCOPED),
        cost_estimate=pl.CostEstimate(
            flops=2 * rows * feats * width,
            bytes_accessed=(rows + width) * feats * 2,
            transcendentals=rows * width,
        ),
    )(*inputs)


def small_call(kernel, name, shape, inputs, pinned):
    n = len(inputs)

    def with_pinned(*refs):
        kernel(*refs[:n], refs[n + len(pinned)])

    out, *pinned = pl.pallas_call(
        with_pinned,
        name=name,
        out_shape=[pltpu.VMEM(shape, inputs[0].dtype)]
        + [pltpu.VMEM(p.shape, p.dtype) for p in pinned],
        in_specs=[VM] * (n + len(pinned)),
        out_specs=[VM] * (1 + len(pinned)),
        input_output_aliases={n + i: 1 + i for i in range(len(pinned))},
        compiler_params=pltpu.CompilerParams(vmem_limit_bytes=SCOPED),
    )(*[in_vmem(a) for a in [*inputs, *pinned]])
    return out, pinned


def join_kernel(first_ref, second_ref, out_ref):
    n = first_ref.shape[0]
    out_ref[:n] = first_ref[...]
    out_ref[n:] = second_ref[...]


def merge_kernel(*refs):
    top, total, labels = merge_parts([r[...] for r in refs[:-1]])
    n = top.shape[0]
    refs[-1][:n] = top
    refs[-1][n : 2 * n] = total
    refs[-1][2 * n :] = labels


def update_kernel(cfg, *refs):
    chips, n_msgs, bm, held_blocks, bn = cfg
    msgs, refs = refs[:n_msgs], refs[n_msgs:]
    other_ref, accum_hbm, logits_ref, x_ref = refs[:4]
    w_ref, acc_ref, out_w, out_acc, out_lse = refs[6:11]
    canon_s, lse_s, label_s, delta_s, grad_s, read_sem, acc_sem, w_sem = refs[11:]
    rows, batch = logits_ref.shape
    feats = x_ref.shape[1]
    blocks = rows // bm

    chip, core, _ = whereabouts(chips)
    rank = lax.axis_index("blk") * lax.axis_size("cls") + lax.axis_index("cls")
    first_class = rank * rows
    top, total, labels = merge_parts([m[...] for m in msgs])
    slab_lse = top + jnp.log(total)
    other = other_ref[...]
    high = jnp.maximum(slab_lse, other)
    lse = high + jnp.log(jnp.exp(slab_lse - high) + jnp.exp(other - high))
    canon_s[:chips] = lse
    canon_s[chips:] = labels
    own = canon_s[pl.ds(chip, 1), :]
    out_lse[...] = jnp.where(core == 0, own[:, : LANES // 2], own[:, LANES // 2 :])
    slots = block_slots(chips)
    for j in range(chips):
        lanes = pl.ds(j * LANES, LANES)
        pair = slots[2 * j : 2 * j + 2]
        lse_s[:, lanes] = jnp.concatenate(
            [one_half(canon_s[pl.ds(owner, 1), :], side) for owner, side in pair], axis=1
        )
        label = jnp.concatenate(
            [one_half(canon_s[pl.ds(chips + owner, 1), :], side) for owner, side in pair], axis=1
        )
        label_s[:, lanes] = label.astype(i32) - first_class

    def make_delta(i, to):
        r0 = pl.multiple_of(i * bm, bm)
        chance = jnp.exp(logits_ref[pl.ds(r0, bm), :] - lse_s[...])
        row = lax.broadcasted_iota(i32, (bm, batch), 0)
        hit = row == (label_s[...] - r0)
        delta_s[to] = jnp.where(hit, chance - 1.0, chance).astype(bf16)

    def rows_of(i):
        return pl.ds(pl.multiple_of(i * bm, bm), bm)

    def read(i):
        slot = lax.rem(i, held_blocks)
        return pltpu.make_async_copy(
            accum_hbm.at[rows_of(i)], acc_ref.at[rows_of(slot)], read_sem.at[slot]
        )

    def writes(i):
        slot = lax.rem(i, held_blocks)
        return (
            pltpu.make_async_copy(
                acc_ref.at[rows_of(slot)], out_acc.at[rows_of(i)], acc_sem.at[slot]
            ),
            pltpu.make_async_copy(
                w_ref.at[rows_of(i)], out_w.at[rows_of(i)], w_sem.at[lax.rem(i, LAG + 1)]
            ),
        )

    make_delta(0, 0)
    grad_s[...] = jnp.zeros_like(grad_s)

    def step(i, carry):
        now = lax.rem(i, 2)
        slot = lax.rem(i, held_blocks)

        @pl.when(i >= held_blocks)
        def _():
            read(i).wait()

        make_delta(jnp.minimum(i + 1, blocks - 1), 1 - now)
        def grad_tile(n):
            grad_s[n % 2] = jnp.dot(
                delta_s[now], x_ref[:, pl.ds(n * bn, bn)], preferred_element_type=f32
            )

        acc_rows, w_rows = acc_ref.at[rows_of(slot)], w_ref.at[rows_of(i)]

        def update_tile(n):
            cols = pl.ds(n * bn, bn)
            for r in range(0, bm, SUB):
                here = pl.ds(r, SUB)
                grad = grad_s[n % 2, here, :]
                new_acc = acc_rows[here, cols] + grad * grad
                acc_rows[here, cols] = new_acc
                root = new_acc * lax.rsqrt(new_acc)
                part = (0.05 * grad) * pltpu.reciprocal(root + 1e-10, approx=True)
                w_rows[here, cols] = (w_rows[here, cols].astype(f32) - part).astype(bf16)

        tiles = feats // bn
        grad_tile(0)
        for n in range(1, tiles):
            grad_tile(n)
            update_tile(n - 1)
        update_tile(tiles - 1)

        @pl.when(i >= LAG)
        def _():
            for copy in writes(i - LAG):
                copy.wait()

            @pl.when(i - LAG + held_blocks < blocks)
            def _():
                read(i - LAG + held_blocks).start()

        for copy in writes(i):
            copy.start()
        return carry

    lax.fori_loop(0, blocks, step, 0)
    for i in range(max(0, blocks - LAG), blocks):
        for copy in writes(i):
            copy.wait()


def update(chips, msgs, other, accum, logits, x, weight_v, acc_v, bm):
    rows, batch = logits.shape
    feats = x.shape[1]
    held_blocks = acc_v.shape[0] // bm
    bn = min(256, feats)
    inputs = [in_vmem(m) for m in msgs] + [other, in_hbm(accum)] + [
        in_vmem(a) for a in (logits, x, weight_v, acc_v)
    ]
    n = len(msgs)
    cfg = (chips, n, bm, held_blocks, bn)
    outs = pl.pallas_call(
        functools.partial(update_kernel, cfg),
        name="update",
        out_shape=[
            pltpu.VMEM(weight_v.shape, bf16),
            pltpu.VMEM(acc_v.shape, f32),
            pltpu.HBM((rows, feats), bf16),
            pltpu.HBM((rows, feats), f32),
            jax.ShapeDtypeStruct((1, LANES // 2), f32),
        ],
        in_specs=[VM] * n + [VM, ANY, VM, VM, VM, VM],
        out_specs=[VM, VM, ANY, ANY, VM],
        input_output_aliases={n + 4: 0, n + 5: 1},
        scratch_shapes=[
            pltpu.VMEM((2 * chips, LANES), f32),
            pltpu.VMEM((1, batch), f32),
            pltpu.VMEM((1, batch), i32),
            pltpu.VMEM((2, bm, batch), bf16),
            pltpu.VMEM((2, bm, bn), f32),
            pltpu.SemaphoreType.DMA((held_blocks,)),
            pltpu.SemaphoreType.DMA((held_blocks,)),
            pltpu.SemaphoreType.DMA((LAG + 1,)),
        ],
        compiler_params=pltpu.CompilerParams(vmem_limit_bytes=SCOPED),
        cost_estimate=pl.CostEstimate(
            flops=2 * rows * feats * batch,
            bytes_accessed=rows * feats * 10,
            transcendentals=rows * batch,
        ),
    )(*inputs)
    return outs[2:]


def exchange_stats(message, pinned, blk_size, cls_size):
    bits_cls = cls_size.bit_length() - 1
    bits = bits_cls + blk_size.bit_length() - 1
    core, y = bits_cls, bits_cls + 1
    rest = [b for b in range(bits) if b not in (core, y, 0)]
    groups = [(core,), (0, y)] + [tuple(rest[i : i + 2]) for i in range(0, len(rest), 2)]
    messages = [message]
    for group in groups:
        if len(messages) > 1:
            message, pinned = small_call(
                merge_kernel, "merge_stats", message.shape, messages, pinned
            )
        messages = [message]
        for pick in range(1, 2 ** len(group)):
            flip = sum(1 << b for at, b in enumerate(group) if pick >> at & 1)
            pairs = [(d, d ^ flip) for d in range(blk_size * cls_size)]
            messages.append(lax.ppermute(message, ("blk", "cls"), pairs))
    return messages, pinned


def body(features, labels, offset, other_lse, weight, accum):
    blk_size, cls_size = lax.axis_size("blk"), lax.axis_size("cls")
    chips = blk_size // 2
    steps = chips // 2
    block, feats = features.shape
    rows = weight.shape[0]
    batch = block * blk_size
    bm = min(256 * 1024 // batch, rows)
    held_rows = min(rows, HELD_BYTES // (feats * 4))

    def swap_cores(x):
        return lax.ppermute(x, "blk", [(d, d ^ 1) for d in range(blk_size)])

    def round_ring(x):
        return lax.ppermute(x, "blk", ring_pairs(chips))

    came = round_ring(features)
    sibling = swap_cores(features)
    *pinned, message = hold(weight, labels, offset, chips, batch, held_rows)
    came, message = lax.optimization_barrier((came, message))
    state = [message, *pinned]
    joined, state[1:] = small_call(
        join_kernel, "join", (2 * block, feats), [sibling, came], state[1:]
    )
    blocks = [features, sibling, came, swap_cores(came)]
    came = round_ring(joined)
    held = 0
    for k in range(steps):
        if k > 0:
            blocks = [came, swap_cores(came)]
            if k < steps - 1:
                came = round_ring(came)
        until = held_rows if k == steps - 1 else min(held_rows, 4 * k * bm)
        state = list(score(k, chips, blocks, accum, weight, (held, until), state))
        held = until
        if k < steps - 1:
            came, state[0] = lax.optimization_barrier((came, state[0]))
    messages, pinned = exchange_stats(state[0], state[1:], blk_size, cls_size)
    weight_v, logits, x, acc_v = pinned
    new_weight, new_accum, lse = update(
        chips, messages, other_lse.reshape(chips, LANES), accum, logits, x, weight_v, acc_v, bm
    )
    return (new_weight, new_accum, lse.reshape(block))


def solution(mesh):
    in_specs = (
        P("blk", None),
        P("blk"),
        P(),
        P(),
        P(("blk", "cls"), None),
        P(("blk", "cls"), None),
    )
    out_specs = (P(("blk", "cls"), None), P(("blk", "cls"), None), P("blk"))
    return jax.shard_map(body, mesh=mesh, in_specs=in_specs, out_specs=out_specs, check_vma=False)
```
